32 devices in a mesh: dp: 16 (over z, y, core), tensor: 2 (over x).
Axes of the slice: x: 2, y: 2, z: 4, core: 2. Of those that a mesh axis runs over, the one named last changes fastest.
Arguments:
- hidden_in: bfloat16 [4608, 768], P(('dp', 'tensor')), may hold values from -6 to 6
- lengths: int32 [16, 3], P('dp'), may hold values from 1 to 192, 288 in all within a row
- routes: int32 [4608, 1], P('dp'), may hold values from 0 to 1; in each aligned block of 288 rows (0 to 287, 288 to 575, ...) at most 192 rows name the same one
- gain_attn: float32 [768], replicated, may hold values from 0.5 to 1.5
- wqkv: bfloat16 [768, 3, 768], P('dp', None, 'tensor'), may hold values from -0.21875 to 0.21875
- wo_t: bfloat16 [768, 768], P('dp', 'tensor'), may hold values from -1.75 to 1.75
- bias_table: float32 [32, 12], replicated, may hold values from -4 to 4
- gain_ffn: float32 [768], replicated, may hold values from 0.5 to 1.5
- router: bfloat16 [768, 2], replicated, may hold values from -0.15625 to 0.15625
- w_up: bfloat16 [768, 2, 3072], P('dp', None, 'tensor'), may hold values from -0.21875 to 0.21875
- w_down_t: bfloat16 [768, 2, 3072], P('dp', None, 'tensor'), may hold values from -0.3125 to 0.3125
- cotangent: bfloat16 [4608, 768], P(('dp', 'tensor')), may hold values from -6 to 6
Outputs:
- out_hidden: bfloat16 [4608, 768], P(('dp', 'tensor'))
- grad_input: bfloat16 [4608, 768], P(('dp', 'tensor'))
- grad_gain_attn: float32 [768], replicated
- grad_wqkv: float32 [768, 3, 768], P('dp', None, 'tensor')
- grad_wo: float32 [768, 768], P('dp', 'tensor')
- grad_bias: float32 [32, 12], replicated
- grad_gain_ffn: float32 [768], replicated
- grad_router: float32 [768, 2], replicated
- grad_up: float32 [768, 2, 3072], P('dp', None, 'tensor')
- grad_down: float32 [768, 2, 3072], P('dp', None, 'tensor')
The draws below stay inside these ranges and needn't reach their ends.
Inputs may be any that keep to these rules, and one draw needn't show every extreme that they name: Each row of lengths holds 3 lengths that sum to 288; the largest is exactly 192. `routes`: in each pack of 288 rows (the rows of one index of dp) at most 192 rows name one expert; in some pack one expert is named by exactly 192 rows.
All inputs are finite; a program needn't handle non-finite values.
Results may differ from the reference program's by a relative error of at most 0.019.
Values may be sent and summed in bfloat16 or wider, within the bound.
A program may use at most 192 MiB of HBM per device.

```python
import math
import jax
import jax.numpy as jnp
import numpy as np
from jax import lax

D = 768
H = 12
HD = 64
FF = 3072
EXPERTS = 2
BUCKETS = 32
SEQS = 3
TOK_DEV = 288
LONGEST = 192
CAP = 192
TOKENS = 4608
N_DP = 16


def strengthened(entries, stream_key, source, target, parts, factor):
    owner, partner = [(jnp.arange(entries.shape[dim]) // (entries.shape[dim] // parts)).reshape([-1 if axis == dim else 1 for axis in range(entries.ndim)]) for dim in (source, target)]
    chosen = jax.random.permutation(stream_key, parts)[partner]
    strong = (owner == chosen) | (owner == (partner + parts // 2) % parts)
    return jnp.where(strong, factor * entries, entries)


def level_of(rng, extent, shards, least, largest):
    gain = 1.0
    for dim, parts in shards:
        steps = jax.random.uniform(jax.random.fold_in(jax.random.fold_in(rng, 6), dim), (parts,), jnp.float32, least / len(shards), largest / len(shards))
        gain = gain * jnp.repeat(jnp.exp(steps), extent[dim] // parts).reshape((-1,) + (1,) * (len(extent) - 1 - dim))
    return gain


def split_up(count, total, limit, slope):
    portions = [(1 << 20) // math.isqrt(rank ** slope) + 1 for rank in range(2, count + 1)]
    surplus, given = total - limit - (count - 1), [1] * (count - 1)
    while surplus > 0:
        candidates = [i for i in range(count - 1) if given[i] < limit]
        whole, left = sum([portions[i] for i in candidates]), surplus
        for i in candidates:
            extra = min(limit - given[i], max(1, left * portions[i] // whole), surplus)
            given[i] = given[i] + extra
            surplus = surplus - extra
    return np.array([limit] + given)


def uneven(own_key, number_of, total, bound, skew):
    if number_of == 2:
        one = jax.random.randint(own_key, (), max(1, total - bound), min(bound, total - 1) + 1)
        return jnp.stack([one, total - one])
    sizes = jnp.asarray(split_up(number_of, total, bound, skew), jnp.int32)
    couples = (number_of - 1) // 2
    source_of, sink = sizes[1:1 + 2 * couples:2], sizes[2:2 + 2 * couples:2]
    margin = jnp.minimum(source_of - 1, bound - sink)
    passed = jax.random.randint(jax.random.fold_in(own_key, 1), (couples,), 0, 1 << 20) % (margin + 1)
    sizes = sizes.at[1:1 + 2 * couples:2].set(source_of - passed).at[2:2 + 2 * couples:2].set(sink + passed)
    return sizes[jax.random.permutation(jax.random.fold_in(own_key, 2), number_of)]


def deal_out(own_key, own, number, rows, count, top, most, lean):
    order = jax.random.permutation(own_key, count)
    packed, common = portions_of(count, rows * top, most, lean, True), portions_of(count, rows * top, most, lean, False)
    places = jnp.arange(count)

    def named(sizes, offset_by):
        used = int((sizes > 0).sum())
        fixed = max(1, used // 4)
        passed = fixed + (places - fixed + offset_by * (used - fixed)) % max(1, count - fixed)
        return jnp.zeros((count,), jnp.int32).at[order[jnp.where(places < fixed, places, passed)]].set(jnp.asarray(sizes, jnp.int32))

    sizes = jnp.where(number % 4 == 0, named(packed, number // 4), named(common, number - number // 4 - 1))
    mixed = jax.random.permutation(jax.random.fold_in(own, 3), count)
    source_of, sink = mixed[0:count // 2 * 2:2], mixed[1:count // 2 * 2:2]
    room = jnp.minimum(sizes[source_of] - 1, most - sizes[sink]) // 2
    room = jnp.where((source_of == order[0]) | (sink == order[0]) | (sizes[sink] == 0), 0, jnp.maximum(room, 0))
    passed = jax.random.randint(jax.random.fold_in(own, 4), (count // 2,), 0, 1 << 20) % (room + 1)
    sizes = sizes.at[source_of].add(-passed).at[sink].add(passed)
    items = jnp.searchsorted(jnp.cumsum(sizes), jnp.arange(rows * top), side="right").astype(jnp.int32)
    grid = items.reshape(top, rows).T
    grid = grid[jax.random.permutation(jax.random.fold_in(own, 1), rows)]
    offset_by = jax.random.randint(jax.random.fold_in(own, 2), (rows, 1), 0, top)
    return jnp.take_along_axis(grid, (jnp.arange(top)[None, :] + offset_by) % top, axis=1)


def portions_of(number_of, total, most, lean, full):
    weights = [(1 << 20) // math.isqrt(standing ** lean) + 1 for standing in range(1, number_of + 1)]
    largest = most if full else min(most, max(-(-total // number_of), total * weights[0] // sum(weights)))
    least = 1 if total - largest >= number_of - 1 else 0
    holding, spare = [largest] + [least] * (number_of - 1), total - largest - least * (number_of - 1)
    while spare > 0:
        movable = [i for i in range(1, number_of) if holding[i] < largest] or [i for i in range(1, number_of) if holding[i] < most]
        mass, budget = sum([weights[i] for i in movable]), spare
        for i in movable:
            extra = min(most - holding[i], max(1, budget * weights[i] // mass), spare)
            holding[i] = holding[i] + extra
            spare = spare - extra
    return np.array(holding)


def normal_values(stream_key, dims, deviation, bound, cuts=(), held_as=jnp.bfloat16):
    drawn = jax.random.normal(stream_key, dims, jnp.float32) * deviation
    if len(cuts) > 0:
        drawn = level_of(stream_key, dims, cuts, -0.22, 0.18) * drawn
    return jnp.clip(drawn, min=-bound, max=bound).astype(held_as)


def bell_draw_with(stream_key, shape, width, most, cuts, heavy, held_as=jnp.bfloat16):
    array = width * jax.random.normal(stream_key, shape, jnp.float32)
    if cuts:
        array = array * level_of(stream_key, shape, cuts, -0.22, 0.18)
    return jnp.clip(strengthened(array, jax.random.fold_in(stream_key, 3), *heavy), -most, most).astype(held_as)


def setup_inputs(seed: int = 0) -> dict:
    splits = jax.random.split(jax.random.key(seed), 13)
    hidden_in = bell_draw_with(splits[0], (TOKENS, D), 1.0, 6.0, ((0, 32),), (0, 1, 32, 2.75))
    lengths = jax.vmap(lambda own: uneven(own, SEQS, TOK_DEV, LONGEST, 2))(jax.random.split(splits[1], N_DP)).reshape((N_DP, SEQS)).astype(jnp.int32)
    routes_keys = jax.random.split(jax.random.fold_in(splits[2], 1), TOKENS // TOK_DEV)
    routes_turns = jax.random.permutation(jax.random.fold_in(splits[2], 3), TOKENS // TOK_DEV)
    routes = jax.vmap(lambda own, number: deal_out(jax.random.fold_in(splits[2], 2), own, number, TOK_DEV, EXPERTS, 1, CAP, 1))(routes_keys, routes_turns).reshape((TOKENS, 1))
    gain_attn = jnp.clip(1.0 + 0.1 * jax.random.normal(splits[3], (D,), jnp.float32), 0.5, 1.5)
    wqkv = normal_values(splits[4], (D, 3, D), D ** -0.5, 0.21875, ((0, 16), (2, 2)))
    wo_t = normal_values(splits[5], (D, D), (D // 64) ** -0.5, 1.75, ((0, 16), (1, 2)))
    bias_table = normal_values(splits[6], (BUCKETS, H), 1.0, 4.0, (), jnp.float32)
    gain_ffn = jnp.clip(1.0 + 0.1 * jax.random.normal(splits[7], (D,), jnp.float32), 0.5, 1.5)
    router = normal_values(splits[8], (D, EXPERTS), (2 * D) ** -0.5, 0.15625)
    w_up = normal_values(splits[9], (D, EXPERTS, FF), D ** -0.5, 0.21875, ((0, 16), (2, 2)))
    w_down_t = normal_values(splits[10], (D, EXPERTS, FF), (FF // 8) ** -0.5, 0.3125, ((0, 16), (2, 2)))
    cotangent = bell_draw_with(splits[11], (TOKENS, D), 1.0, 6.0, ((0, 32),), (0, 1, 32, 2.75))
    return {"hidden_in": hidden_in, "lengths": lengths, "routes": routes, "gain_attn": gain_attn, "wqkv": wqkv, "wo_t": wo_t, "bias_table": bias_table, "gain_ffn": gain_ffn, "router": router, "w_up": w_up, "w_down_t": w_down_t, "cotangent": cotangent}


@jax.custom_vjp
def low(v):
    return lax.optimization_barrier(v.astype(jnp.bfloat16)).astype(jnp.float32)

@jax.custom_vjp
def low_back(v):
    return v

def low_keep(v):
    return (low(v), None)

def low_pass(kept, grad):
    return (grad,)

def back_keep(v):
    return (v, None)

def back_low(kept, grad):
    return (low(grad),)
low.defvjp(low_keep, low_pass)
low_back.defvjp(back_keep, back_low)
epsilon = 1e-06
bucket_limits = (12, 16, 23, 32, 46, 64, 91)
highest = lax.Precision.HIGHEST

def normalize(values, gains):
    return values * lax.rsqrt(lax.optimization_barrier(jnp.mean(values * values, axis=-1, keepdims=True)) + epsilon) * gains

def rel_bucket(offsets):
    distance = jnp.abs(offsets)
    beyond = jnp.full(offsets.shape, 8, jnp.int32)
    for limit_value in bucket_limits:
        beyond = beyond + (distance >= limit_value).astype(jnp.int32)
    within = jnp.where(distance < 8, distance, beyond).astype(jnp.int32)
    return within + jnp.where(offsets > 0, 16, 0).astype(jnp.int32)

def document_ids(length_row, count):
    bounds = jnp.cumsum(length_row).astype(jnp.int32)
    positions = jnp.arange(count, dtype=jnp.int32)
    return lax.optimization_barrier(jnp.sum((positions[:, None] >= bounds[None, :]).astype(jnp.int32), axis=1))

def slot_ids(route_row):
    onehot = (route_row[:, None] == jnp.arange(EXPERTS, dtype=jnp.int32)[None, :]).astype(jnp.int32)
    before = jnp.cumsum(onehot, axis=0) - onehot
    return (route_row * CAP + lax.optimization_barrier(jnp.sum(before * onehot, axis=1))).astype(jnp.int32)

def softmax_rows(values):
    shifted = jnp.exp(values - lax.optimization_barrier(jnp.max(values, axis=-1, keepdims=True)))
    return shifted / lax.optimization_barrier(jnp.sum(shifted, axis=-1, keepdims=True))

def pack_forward(weights, pack_input, doc_ids, route_row):
    gain_attn, wqkv, wo_t, bias_table, gain_ffn, router, w_up, w_down_t = weights
    pack_rows = pack_input.shape[0]
    norm_one = low(normalize(pack_input, gain_attn))
    projected = jnp.einsum('td,dcf->tcf', norm_one, wqkv, precision=highest)
    projected = low_back(low(projected)).reshape(pack_rows, 3, H, HD)
    queries = projected[:, 0]
    keys_all = projected[:, 1]
    values_all = projected[:, 2]
    positions = jnp.arange(pack_rows, dtype=jnp.int32)
    buckets = rel_bucket(positions[None, :] - positions[:, None])
    bias_rows = jnp.transpose(jnp.take(bias_table, buckets, axis=0), (2, 0, 1))
    same_doc = doc_ids[:, None] == doc_ids[None, :]
    raw_scores = jnp.einsum('qhd,khd->hqk', queries, keys_all, precision=highest) * HD ** (-0.5)
    scores = jnp.where(same_doc[None], low_back(raw_scores) + bias_rows, -1e+30)
    probs = softmax_rows(scores)
    mixed = jnp.einsum('hqk,khd->qhd', low(probs), values_all, precision=highest).reshape(pack_rows, D)
    mixed = low_back(low(mixed))
    attended = low_back(jnp.einsum('tk,dk->td', mixed, wo_t, precision=highest))
    middle = pack_input + attended
    norm_two = low(normalize(middle, gain_ffn))
    router_probs = softmax_rows(jnp.dot(norm_two, router, precision=highest))
    chosen = route_row[:, None] == jnp.arange(EXPERTS, dtype=jnp.int32)[None, :]
    gate_probs = lax.optimization_barrier(jnp.sum(jnp.where(chosen, router_probs, 0.0), axis=-1))
    slot_index = slot_ids(route_row)
    dispatched = jnp.zeros((EXPERTS * CAP, D), jnp.float32).at[slot_index].set(norm_two).reshape(EXPERTS, CAP, D)
    pre_act = low_back(jnp.einsum('ecd,def->ecf', dispatched, w_up, precision=highest))
    hidden_act = low(jax.nn.gelu(pre_act))
    expert_out = jnp.einsum('ecf,def->ecd', hidden_act, w_down_t, precision=highest)
    expert_out = low_back(expert_out).reshape(EXPERTS * CAP, D)
    return middle + gate_probs[:, None] * expert_out[slot_index]

def reference(hidden_in, lengths, routes, gain_attn, wqkv, wo_t, bias_table, gain_ffn, router, w_up, w_down_t, cotangent):
    weights = (gain_attn, wqkv.astype(jnp.float32), wo_t.astype(jnp.float32), bias_table, gain_ffn, router.astype(jnp.float32), w_up.astype(jnp.float32), w_down_t.astype(jnp.float32))
    pack_inputs = hidden_in.astype(jnp.float32).reshape(N_DP, TOK_DEV, D)
    pack_grads = cotangent.astype(jnp.float32).reshape(N_DP, TOK_DEV, D)
    route_rows = routes.reshape(N_DP, TOK_DEV)

    def one_pack(totals, pack_items):
        pack_input, pack_grad, length_row, route_row = pack_items
        doc_ids = document_ids(length_row, TOK_DEV)

        def forward(weight_tuple, rows):
            return pack_forward(weight_tuple, rows, doc_ids, route_row)
        result, pullback = jax.vjp(forward, weights, pack_input)
        weight_grads, input_grad = pullback(pack_grad)
        totals = jax.tree.map(lambda summed, addend: summed + addend, totals, weight_grads)
        return (totals, (result, input_grad))
    start_grads = jax.tree.map(jnp.zeros_like, weights)
    totals, outputs = lax.scan(one_pack, start_grads, (pack_inputs, pack_grads, lengths, route_rows))
    results, input_grads = outputs
    out_hidden = results.reshape(TOKENS, D).astype(jnp.bfloat16)
    grad_input = input_grads.reshape(TOKENS, D).astype(jnp.bfloat16)
    return (out_hidden, grad_input, totals[0], totals[1], totals[2], totals[3], totals[4], totals[5], totals[6], totals[7])
```

```python
import jax
import jax.numpy as jnp
import numpy as np
from jax import lax
from jax.experimental import pallas as pl
from jax.experimental.pallas import tpu as pltpu
from jax.sharding import PartitionSpec as P

HD = 64
EXPERTS = 2
BUCKETS = 32
CAP = 192

epsilon = 1e-06
bucket_limits = (12, 16, 23, 32, 46, 64, 91)
highest = lax.Precision.HIGHEST
f32 = jnp.float32
bf16 = jnp.bfloat16


def normalize(values, gains):
    return values * lax.rsqrt(jnp.mean(values * values, axis=-1, keepdims=True) + epsilon) * gains


def bucket_onehot(offsets):
    distance = np.abs(offsets)
    beyond = 8 + sum((distance >= limit).astype(np.int32) for limit in bucket_limits)
    buckets = np.where(distance < 8, distance, beyond) + np.where(offsets > 0, 16, 0)
    return jnp.asarray(buckets[:, None] == np.arange(BUCKETS)[None, :], f32)


def dot_nn(a, b):
    return lax.dot_general(a, b, (((1,), (0,)), ((), ())), preferred_element_type=f32)


def dot_nt(a, b):
    return lax.dot_general(a, b, (((1,), (1,)), ((), ())), preferred_element_type=f32)


def dot_tn(a, b):
    return lax.dot_general(a, b, (((0,), (0,)), ((), ())), preferred_element_type=f32)


def head_probs(q, k, v_ref, same, h, rows, wide):
    raw = dot_nt(q, k) * HD ** (-0.5)
    spread = jnp.broadcast_to(v_ref[h : h + 1, :], (rows, wide))
    bias = pltpu.roll(spread, 0, 1, stride=1, stride_axis=0)[:, :rows]
    scores = jnp.where(same, raw + bias, -1e30)
    shifted = jnp.exp(scores - jnp.max(scores, axis=-1, keepdims=True))
    return shifted / jnp.sum(shifted, axis=-1, keepdims=True)


def forward_kernel(heads, rows, wide, qkv_ref, v_ref, dc_ref, dr_ref, out_ref):
    same = dc_ref[...] == dr_ref[...]
    width = heads * HD
    for h in range(heads):
        cut = slice(h * HD, (h + 1) * HD)
        q = qkv_ref[:, h * HD : (h + 1) * HD]
        k = qkv_ref[:, width + h * HD : width + (h + 1) * HD]
        v = qkv_ref[:, 2 * width + h * HD : 2 * width + (h + 1) * HD]
        probs = head_probs(q, k, v_ref, same, h, rows, wide)
        out_ref[:, cut] = dot_nn(probs.astype(bf16), v).astype(bf16)


def backward_kernel(heads, rows, wide, qkv_ref, gm_ref, v_ref, dc_ref, dr_ref, gp_ref, diag_ref):
    same = dc_ref[...] == dr_ref[...]
    width = heads * HD
    flip = (
        lax.broadcasted_iota(jnp.int32, (rows, rows), 0)
        + lax.broadcasted_iota(jnp.int32, (rows, rows), 1)
        == rows - 1
    ).astype(f32).astype(bf16)
    diag_ref[...] = jnp.zeros_like(diag_ref)
    for h in range(heads):
        q = qkv_ref[:, h * HD : (h + 1) * HD]
        k = qkv_ref[:, width + h * HD : width + (h + 1) * HD]
        v = qkv_ref[:, 2 * width + h * HD : 2 * width + (h + 1) * HD]
        g = gm_ref[:, h * HD : (h + 1) * HD]
        probs = head_probs(q, k, v_ref, same, h, rows, wide)
        gv = dot_tn(probs.astype(bf16), g)
        gprobs = dot_nt(g, v)
        ds = probs * (gprobs - jnp.sum(probs * gprobs, axis=-1, keepdims=True))
        low = ds.astype(bf16)
        gq = dot_nn(low, k) * HD ** (-0.5)
        gk = dot_tn(low, q) * HD ** (-0.5)
        gp_ref[:, h * HD : (h + 1) * HD] = gq.astype(bf16)
        gp_ref[:, width + h * HD : width + (h + 1) * HD] = gk.astype(bf16)
        gp_ref[:, 2 * width + h * HD : 2 * width + (h + 1) * HD] = gv.astype(bf16)
        turned = dot_nn(flip, low)
        padded = jnp.concatenate([turned, jnp.zeros((rows, wide - rows), f32)], axis=1)
        rolled = pltpu.roll(padded, 0, 1, stride=1, stride_axis=0)
        diag_ref[h : h + 1, :] = jnp.sum(rolled, axis=0, keepdims=True)


def call_kernel(body, outs, flops, *operands):
    return pl.pallas_call(
        body,
        out_shape=outs,
        in_specs=[pl.BlockSpec(memory_space=pltpu.VMEM)] * len(operands),
        out_specs=jax.tree.map(lambda _: pl.BlockSpec(memory_space=pltpu.VMEM), outs),
        compiler_params=pltpu.CompilerParams(vmem_limit_bytes=40 * 2**20),
        cost_estimate=pl.CostEstimate(flops=flops, bytes_accessed=2**21, transcendentals=2**20),
    )(*operands)


def make_links(dp):
    def by(mask):
        return [(i, i ^ mask) for i in range(dp)]

    ring = [(i, (i + 4) % dp) for i in range(dp)]

    def move(x, perm):
        return lax.ppermute(x, "dp", perm)

    def gather(own):
        if dp != 16:
            full = lax.all_gather(own, "dp", axis=0, tiled=True)
            return full[: full.shape[0] // 2], full[full.shape[0] // 2 :]
        held, sides = [own], [move(own, by(2))]
        for _ in range(3):
            held.append(move(held[-1], ring))
            sides.append(move(held[-1], by(2)))
        near = jnp.concatenate(held + sides, axis=0)
        return near, move(near, by(1))

    def add(a, b):
        return a.astype(f32) + b.astype(f32)

    def scatter(keep, send):
        if dp != 16:
            return lax.psum_scatter(
                jnp.concatenate([keep, send], axis=0), "dp", scatter_dimension=0, tiled=True
            ).astype(f32)
        got = move(send.astype(bf16), by(1))
        half = keep.shape[0] // 2
        far = add(keep[half:], got[half:]).astype(bf16)
        near = add(keep[:half], got[:half])
        got = move(far, by(2))
        near = add(near, got)
        part = half // 4
        chunk = near[part : 2 * part].astype(bf16)
        for step in range(3):
            got = move(chunk, ring)
            at = (step + 2) % 4
            total = add(near[at * part : (at + 1) * part], got)
            chunk = total.astype(bf16)
        return total

    def total(x):
        if dp != 16:
            return lax.psum(x, ("dp", "tensor"))
        x = x + lax.ppermute(x, "tensor", [(0, 1), (1, 0)])
        for mask in (1, 2, 4, 8):
            x = x + move(x, by(mask))
        return x

    return gather, scatter, total


def shards(
    hidden_in,
    lengths,
    routes,
    gain_attn,
    wqkv,
    wo_t,
    bias_table,
    gain_ffn,
    router,
    w_up,
    w_down_t,
    cotangent,
):
    dp = lax.axis_size("dp")
    gather, scatter, total = make_links(dp)
    rank = lax.axis_index("tensor")
    half_rows = hidden_in.shape[0]
    rows = routes.shape[0]
    width = hidden_in.shape[1]
    mid = width // 2
    cols = wqkv.shape[2]
    heads = cols // HD
    hidden = w_up.shape[2]
    depth = wqkv.shape[0]
    slot_count = EXPERTS * CAP
    wide = 128 * (-(-2 * rows // 128))

    def swap(x):
        return lax.ppermute(x, "tensor", [(0, 1), (1, 0)])

    def whole_rows(own):
        other = swap(own)
        return jnp.where(
            rank == 0, jnp.concatenate([own, other]), jnp.concatenate([other, own])
        )

    def own_rows(x, who):
        return lax.dynamic_slice_in_dim(x, who * half_rows, half_rows, 0)

    attn_own = jnp.concatenate([wqkv.reshape(depth, 3 * cols), wo_t], axis=1)
    attn_w = gather(attn_own)
    up_w = gather(w_up.reshape(depth, EXPERTS * hidden))
    down_w = gather(w_down_t.reshape(depth, EXPERTS * hidden))

    place = jnp.arange(width, dtype=jnp.int32)
    if dp == 16:
        me = lax.axis_index("dp")
        z, y, core = me // 4, (me // 2) % 2, me % 2
        from_core = (core + place // mid) % 2
        from_y = (y + (place // (mid // 2)) % 2) % 2
        from_z = (z + 4 - (place // depth) % 4) % 4
        origin = (from_z * 4 + from_y * 2 + from_core) * depth + place % depth
    else:
        origin = place
    to_here = (place[:, None] == origin[None, :]).astype(bf16)

    hid = dot_nn(whole_rows(hidden_in), to_here)
    cot = dot_nn(whole_rows(cotangent), to_here)
    vectors = jnp.concatenate(
        [gain_attn[None], gain_ffn[None], router.astype(f32).T], axis=0
    )
    vectors = jnp.dot(vectors, to_here.astype(f32), precision=highest)
    gain_one, gain_two, router_here = vectors[0], vectors[1], vectors[2:].astype(bf16)

    positions = jnp.arange(rows, dtype=jnp.int32)
    first, second = lengths[0, 0], lengths[0, 0] + lengths[0, 1]
    docs = (
        (positions >= first).astype(jnp.int32)
        + (positions >= second).astype(jnp.int32)
        + (positions >= second + lengths[0, 2]).astype(jnp.int32)
    )
    doc_col, doc_row = docs[:, None], docs[None, :]
    table_cols = lax.dynamic_slice_in_dim(bias_table, rank * heads, heads, 1)
    turn = np.arange(wide)
    spread = bucket_onehot(np.where(turn < rows, turn, turn - wide))
    offset_vals = jnp.dot(table_cols.T, spread.T, precision=highest)

    norm_one = normalize(hid, gain_one).astype(bf16)
    projected = dot_nn(norm_one[:, :mid], attn_w[0][:, : 3 * cols])
    projected = projected + dot_nn(norm_one[:, mid:], attn_w[1][:, : 3 * cols])
    projected = projected.astype(bf16)
    flops = 2 * heads * rows * rows * HD
    mixed = call_kernel(
        lambda *refs: forward_kernel(heads, rows, wide, *refs),
        jax.ShapeDtypeStruct((rows, cols), bf16),
        2 * flops,
        projected,
        offset_vals,
        doc_col,
        doc_row,
    )
    out_w = [w[:, 3 * cols :] for w in attn_w]
    attended_part = jnp.concatenate([dot_nt(mixed, w) for w in out_w], axis=1).astype(bf16)
    middle = hid + (attended_part.astype(f32) + swap(attended_part).astype(f32))

    norm_two = normalize(middle, gain_two).astype(bf16)
    logits = dot_nt(norm_two, router_here)
    shifted = jnp.exp(logits - jnp.max(logits, axis=-1, keepdims=True))
    router_probs = shifted / jnp.sum(shifted, axis=-1, keepdims=True)
    chosen = routes == jnp.arange(EXPERTS, dtype=jnp.int32)[None, :]
    gate = jnp.sum(jnp.where(chosen, router_probs, 0.0), axis=-1, keepdims=True)
    earlier = (positions[:, None] < positions[None, :]) & (routes == routes[:, 0][None, :])
    slot_index = routes[:, 0] * CAP + jnp.sum(earlier.astype(jnp.int32), axis=0)
    dispatch = (
        slot_index[None, :] == jnp.arange(slot_count, dtype=jnp.int32)[:, None]
    ).astype(bf16)

    def expert_cut(pair, e):
        return [w[:, e * hidden : (e + 1) * hidden] for w in pair]

    up_e = [expert_cut(up_w, e) for e in range(EXPERTS)]
    down_e = [expert_cut(down_w, e) for e in range(EXPERTS)]

    def into(x, pair):
        return dot_nn(x[:, :mid], pair[0]) + dot_nn(x[:, mid:], pair[1])

    def out_of(x, pair):
        return jnp.concatenate([dot_nt(x, w) for w in pair], axis=1)

    def to_tokens(parts):
        return dot_tn(dispatch, jnp.concatenate(parts, axis=0)).astype(bf16)

    dispatched = dot_nn(dispatch, norm_two).astype(bf16)
    scaled_grad = (gate * cot).astype(bf16)
    grad_slots = dot_nn(dispatch, scaled_grad).astype(bf16)
    disp_e = [dispatched[e * CAP : (e + 1) * CAP] for e in range(EXPERTS)]
    slots_e = [grad_slots[e * CAP : (e + 1) * CAP] for e in range(EXPERTS)]

    hidden_act, grad_pre = [], []
    for e in range(EXPERTS):
        value, back = jax.vjp(jax.nn.gelu, into(disp_e[e], up_e[e]))
        hidden_act.append(value.astype(bf16))
        grad_pre.append(back(into(slots_e[e], down_e[e]))[0].astype(bf16))
    grad_rows = to_tokens([out_of(grad_pre[e], up_e[e]).astype(bf16) for e in range(EXPERTS)])
    token_part = to_tokens([out_of(hidden_act[e], down_e[e]).astype(bf16) for e in range(EXPERTS)])
    routed = token_part.astype(f32) + swap(token_part).astype(f32)
    grad_rows = grad_rows.astype(f32) + swap(grad_rows).astype(f32)

    def weight_grad(left, right):
        return scatter(
            dot_tn(left[:, :mid], right).astype(bf16), dot_tn(left[:, mid:], right).astype(bf16)
        )

    grad_up = jnp.stack([weight_grad(disp_e[e], grad_pre[e]) for e in range(EXPERTS)], axis=1)
    grad_down = jnp.stack([weight_grad(slots_e[e], hidden_act[e]) for e in range(EXPERTS)], axis=1)

    out_rows = own_rows(middle + gate * routed, rank).astype(bf16)
    out_hidden = dot_nt(out_rows, to_here).astype(bf16)
    grad_gate = jnp.sum(cot * routed, axis=-1, keepdims=True)
    picked = jnp.where(chosen, grad_gate, 0.0)
    grad_logits = router_probs * (picked - gate * grad_gate)
    router_wide = router_here.astype(f32)
    grad_norm_two = grad_rows + sum(
        grad_logits[:, e : e + 1] * router_wide[e : e + 1] for e in range(EXPERTS)
    )
    grad_router_here = jnp.stack(
        [
            jnp.sum(norm_two.astype(f32) * grad_logits[:, e : e + 1], axis=0)
            for e in range(EXPERTS)
        ]
    )
    grad_middle_norm, grad_gain_ffn = jax.vjp(normalize, middle, gain_two)[1](grad_norm_two)
    grad_middle = cot + grad_middle_norm

    grad_attended = grad_middle.astype(bf16)
    grad_mixed = into(grad_attended, out_w).astype(bf16)
    grad_projected, diagonals = call_kernel(
        lambda *refs: backward_kernel(heads, rows, wide, *refs),
        (
            jax.ShapeDtypeStruct((rows, 3 * cols), bf16),
            jax.ShapeDtypeStruct((8, wide), f32),
        ),
        6 * flops,
        projected,
        grad_mixed,
        offset_vals,
        doc_col,
        doc_row,
    )
    grad_rows_one = out_of(grad_projected, [w[:, : 3 * cols] for w in attn_w]).astype(bf16)
    arrived = swap(own_rows(grad_rows_one, 1 - rank))
    grad_norm_one = own_rows(grad_rows_one, rank).astype(f32) + arrived.astype(f32)
    grad_input_norm, grad_gain_attn = jax.vjp(normalize, own_rows(hid, rank), gain_one)[1](
        grad_norm_one
    )
    grad_input = (own_rows(grad_middle, rank) + grad_input_norm).astype(bf16)
    grad_input = dot_nt(grad_input, to_here).astype(bf16)

    attention_sums = scatter(
        *[
            jnp.concatenate(
                [dot_tn(norm_one[:, cut], grad_projected), dot_tn(grad_attended[:, cut], mixed)],
                axis=1,
            ).astype(bf16)
            for cut in (slice(0, mid), slice(mid, width))
        ]
    )
    grad_wqkv = attention_sums[:, : 3 * cols].reshape(depth, 3, cols)
    grad_wo = attention_sums[:, 3 * cols :]

    small = jnp.concatenate(
        [grad_gain_attn[None], 0.5 * grad_gain_ffn[None], 0.5 * grad_router_here], axis=0
    )
    small = lax.dot_general(
        small, to_here.astype(f32), (((1,), (1,)), ((), ())), precision=highest
    )
    by_bucket = bucket_onehot(turn - (rows - 1))
    grad_table = jnp.dot(by_bucket.T, diagonals[:heads].T, precision=highest)
    table_full = lax.dynamic_update_slice_in_dim(
        jnp.zeros(bias_table.shape, f32), grad_table, rank * heads, 1
    )
    flat = table_full.reshape(1, -1)
    flat = jnp.pad(flat, ((0, 0), (0, width - flat.shape[1])))
    sums = total(jnp.concatenate([small, flat], axis=0))
    grad_bias = sums[4, : table_full.size].reshape(bias_table.shape)
    return (
        out_hidden,
        grad_input,
        sums[0],
        grad_wqkv,
        grad_wo,
        grad_bias,
        sums[1],
        sums[2:4].T,
        grad_up,
        grad_down,
    )


def solution(mesh):
    placed = (
        P(("dp", "tensor"), None),
        P("dp", None),
        P("dp", None),
        P(),
        P("dp", None, "tensor"),
        P("dp", "tensor"),
        P(),
        P(),
        P(),
        P("dp", None, "tensor"),
        P("dp", None, "tensor"),
        P(("dp", "tensor"), None),
    )
    return jax.shard_map(
        shards,
        mesh=mesh,
        in_specs=placed,
        out_specs=(
            P(("dp", "tensor"), None),
            P(("dp", "tensor"), None),
            P(),
            P("dp", None, "tensor"),
            P("dp", "tensor"),
            P(),
            P(),
            P(),
            P("dp", None, "tensor"),
            P("dp", None, "tensor"),
        ),
        check_vma=False,
    )
```

```python
import jax
import jax.numpy as jnp
import numpy as np
from jax import lax
from jax.experimental import pallas as pl
from jax.experimental.pallas import tpu as pltpu
from jax.sharding import PartitionSpec as P

HD = 64
EXPERTS = 2
BUCKETS = 32
CAP = 192

epsilon = 1e-06
bucket_limits = (12, 16, 23, 32, 46, 64, 91)
highest = lax.Precision.HIGHEST
f32 = jnp.float32
bf16 = jnp.bfloat16


def normalize(values, gains):
    return values * lax.rsqrt(jnp.mean(values * values, axis=-1, keepdims=True) + epsilon) * gains


def bucket_onehot(offsets):
    distance = np.abs(offsets)
    beyond = 8 + sum((distance >= limit).astype(np.int32) for limit in bucket_limits)
    buckets = np.where(distance < 8, distance, beyond) + np.where(offsets > 0, 16, 0)
    return jnp.asarray(buckets[:, None] == np.arange(BUCKETS)[None, :], f32)


def dot_nn(a, b):
    return lax.dot_general(a, b, (((1,), (0,)), ((), ())), preferred_element_type=f32)


def dot_nt(a, b):
    return lax.dot_general(a, b, (((1,), (1,)), ((), ())), preferred_element_type=f32)


def dot_tn(a, b):
    return lax.dot_general(a, b, (((0,), (0,)), ((), ())), preferred_element_type=f32)


def head_probs(q, k, v_ref, same, h, rows, wide):
    raw = dot_nt(q, k) * HD ** (-0.5)
    spread = jnp.broadcast_to(v_ref[h : h + 1, :], (rows, wide))
    bias = pltpu.roll(spread, 0, 1, stride=1, stride_axis=0)[:, :rows]
    scores = jnp.where(same, raw + bias, -1e30)
    shifted = jnp.exp(scores - jnp.max(scores, axis=-1, keepdims=True))
    return shifted / jnp.sum(shifted, axis=-1, keepdims=True)


def forward_kernel(heads, rows, wide, qkv_ref, v_ref, dc_ref, dr_ref, out_ref):
    same = dc_ref[...] == dr_ref[...]
    width = heads * HD
    for h in range(heads):
        cut = slice(h * HD, (h + 1) * HD)
        q = qkv_ref[:, h * HD : (h + 1) * HD]
        k = qkv_ref[:, width + h * HD : width + (h + 1) * HD]
        v = qkv_ref[:, 2 * width + h * HD : 2 * width + (h + 1) * HD]
        probs = head_probs(q, k, v_ref, same, h, rows, wide)
        out_ref[:, cut] = dot_nn(probs.astype(bf16), v).astype(bf16)


def backward_kernel(heads, rows, wide, qkv_ref, gm_ref, v_ref, dc_ref, dr_ref, gp_ref, diag_ref):
    same = dc_ref[...] == dr_ref[...]
    width = heads * HD
    flip = (
        lax.broadcasted_iota(jnp.int32, (rows, rows), 0)
        + lax.broadcasted_iota(jnp.int32, (rows, rows), 1)
        == rows - 1
    ).astype(f32).astype(bf16)
    diag_ref[...] = jnp.zeros_like(diag_ref)
    for h in range(heads):
        q = qkv_ref[:, h * HD : (h + 1) * HD]
        k = qkv_ref[:, width + h * HD : width + (h + 1) * HD]
        v = qkv_ref[:, 2 * width + h * HD : 2 * width + (h + 1) * HD]
        g = gm_ref[:, h * HD : (h + 1) * HD]
        probs = head_probs(q, k, v_ref, same, h, rows, wide)
        gv = dot_tn(probs.astype(bf16), g)
        gprobs = dot_nt(g, v)
        ds = probs * (gprobs - jnp.sum(probs * gprobs, axis=-1, keepdims=True))
        low = ds.astype(bf16)
        gq = dot_nn(low, k) * HD ** (-0.5)
        gk = dot_tn(low, q) * HD ** (-0.5)
        gp_ref[:, h * HD : (h + 1) * HD] = gq.astype(bf16)
        gp_ref[:, width + h * HD : width + (h + 1) * HD] = gk.astype(bf16)
        gp_ref[:, 2 * width + h * HD : 2 * width + (h + 1) * HD] = gv.astype(bf16)
        turned = dot_nn(flip, low)
        padded = jnp.concatenate([turned, jnp.zeros((rows, wide - rows), f32)], axis=1)
        rolled = pltpu.roll(padded, 0, 1, stride=1, stride_axis=0)
        diag_ref[h : h + 1, :] = jnp.sum(rolled, axis=0, keepdims=True)


def call_kernel(body, outs, flops, *operands):
    return pl.pallas_call(
        body,
        out_shape=outs,
        in_specs=[pl.BlockSpec(memory_space=pltpu.VMEM)] * len(operands),
        out_specs=jax.tree.map(lambda _: pl.BlockSpec(memory_space=pltpu.VMEM), outs),
        compiler_params=pltpu.CompilerParams(vmem_limit_bytes=40 * 2**20),
        cost_estimate=pl.CostEstimate(flops=flops, bytes_accessed=2**21, transcendentals=2**20),
    )(*operands)


def tie(x, *others):
    return lax.optimization_barrier((x,) + others)[0]


def add(a, b):
    return a.astype(f32) + b.astype(f32)


def make_links(dp):
    def by(mask):
        return [(i, i ^ mask) for i in range(dp)]

    ring = [(i, (i + 4) % dp) for i in range(dp)]

    def move(x, perm):
        return lax.ppermute(x, "dp", perm)

    def ring_step(x):
        return move(x, ring)

    def across(x):
        return move(x, by(2))

    def core(x):
        return move(x, by(1))

    return ring_step, across, core, total_of(dp, move, by)


def total_of(dp, move, by):
    def total(x):
        if dp != 16:
            return lax.psum(x, ("dp", "tensor"))
        x = x + lax.ppermute(x, "tensor", [(0, 1), (1, 0)])
        for mask in (1, 2, 4, 8):
            x = x + move(x, by(mask))
        return x

    return total


def shards(
    hidden_in,
    lengths,
    routes,
    gain_attn,
    wqkv,
    wo_t,
    bias_table,
    gain_ffn,
    router,
    w_up,
    w_down_t,
    cotangent,
):
    dp = lax.axis_size("dp")
    ring_step, across, core_swap, total = make_links(dp)
    small_slice = dp == 16
    rank = lax.axis_index("tensor")
    half_rows = hidden_in.shape[0]
    rows = routes.shape[0]
    width = hidden_in.shape[1]
    mid = width // 2
    cols = wqkv.shape[2]
    heads = cols // HD
    hidden = w_up.shape[2]
    depth = wqkv.shape[0]
    slot_count = EXPERTS * CAP
    wide = 128 * (-(-2 * rows // 128))

    def swap(x):
        return lax.ppermute(x, "tensor", [(0, 1), (1, 0)])

    def whole_rows(own):
        other = swap(own)
        return jnp.where(
            rank == 0, jnp.concatenate([own, other]), jnp.concatenate([other, own])
        )

    def own_rows(x, who):
        return lax.dynamic_slice_in_dim(x, who * half_rows, half_rows, 0)

    attn_own = jnp.concatenate([wqkv.reshape(depth, 3 * cols), wo_t], axis=1)
    experts_own = jnp.concatenate(
        [w_up.reshape(depth, EXPERTS * hidden), w_down_t.reshape(depth, EXPERTS * hidden)], axis=1
    )
    parts = EXPERTS * hidden
    if small_slice:
        held, sides = [attn_own], [across(attn_own)]
        for step in range(3):
            held.append(ring_step(held[-1]))
            sides.append(across(held[-1]))
        near = jnp.concatenate(held + sides, axis=0)
        attn_w = (near, core_swap(near))
        begun = tie(experts_own, held[1])
        big_held, big_sides = [begun, ring_step(begun)], [across(begun)]
        big_held[1], big_sides[0], _ = lax.optimization_barrier(
            (big_held[1], big_sides[0], attn_w[1])
        )
        for step in range(2):
            big_held.append(ring_step(big_held[-1]))
            big_sides.append(across(big_held[-2]))
        big_sides.append(across(big_held[-1]))
        pieces = big_held + big_sides
        near_up = jnp.concatenate([p[:, :parts] for p in pieces], axis=0)
        near_down = jnp.concatenate([p[:, parts:] for p in pieces], axis=0)
        up_w = (near_up, core_swap(near_up))
        down_w = (near_down, core_swap(near_down))
    else:
        attn_all = lax.all_gather(attn_own, "dp", axis=0, tiled=True)
        experts_all = lax.all_gather(experts_own, "dp", axis=0, tiled=True)
        attn_w = (attn_all[:mid], attn_all[mid:])
        up_w = (experts_all[:mid, :parts], experts_all[mid:, :parts])
        down_w = (experts_all[:mid, parts:], experts_all[mid:, parts:])

    place = jnp.arange(width, dtype=jnp.int32)
    if small_slice:
        me = lax.axis_index("dp")
        z, y, core = me // 4, (me // 2) % 2, me % 2
        from_core = (core + place // mid) % 2
        from_y = (y + (place // (mid // 2)) % 2) % 2
        from_z = (z + 4 - (place // depth) % 4) % 4
        origin = (from_z * 4 + from_y * 2 + from_core) * depth + place % depth
    else:
        origin = place
    to_here = (place[:, None] == origin[None, :]).astype(bf16)

    hid = dot_nn(whole_rows(hidden_in), to_here)
    cot = dot_nn(whole_rows(cotangent), to_here)
    vectors = jnp.concatenate(
        [gain_attn[None], gain_ffn[None], router.astype(f32).T], axis=0
    )
    vectors = jnp.dot(vectors, to_here.astype(f32), precision=highest)
    gain_one, gain_two, router_here = vectors[0], vectors[1], vectors[2:].astype(bf16)

    positions = jnp.arange(rows, dtype=jnp.int32)
    first, second = lengths[0, 0], lengths[0, 0] + lengths[0, 1]
    docs = (
        (positions >= first).astype(jnp.int32)
        + (positions >= second).astype(jnp.int32)
        + (positions >= second + lengths[0, 2]).astype(jnp.int32)
    )
    doc_col, doc_row = docs[:, None], docs[None, :]
    table_cols = lax.dynamic_slice_in_dim(bias_table, rank * heads, heads, 1)
    turn = np.arange(wide)
    spread = bucket_onehot(np.where(turn < rows, turn, turn - wide))
    offset_vals = jnp.dot(table_cols.T, spread.T, precision=highest)

    norm_one = normalize(hid, gain_one).astype(bf16)
    projected = dot_nn(norm_one[:, :mid], attn_w[0][:, : 3 * cols])
    projected = projected + dot_nn(norm_one[:, mid:], attn_w[1][:, : 3 * cols])
    projected = projected.astype(bf16)
    mixed = call_kernel(
        lambda *refs: forward_kernel(heads, rows, wide, *refs),
        jax.ShapeDtypeStruct((rows, cols), bf16),
        5 * 10**9,
        projected,
        offset_vals,
        doc_col,
        doc_row,
    )
    out_w = [w[:, 3 * cols :] for w in attn_w]
    attended_part = jnp.concatenate([dot_nt(mixed, w) for w in out_w], axis=1).astype(bf16)
    middle = hid + (attended_part.astype(f32) + swap(attended_part).astype(f32))

    norm_two = normalize(middle, gain_two).astype(bf16)
    logits = dot_nt(norm_two, router_here)
    shifted = jnp.exp(logits - jnp.max(logits, axis=-1, keepdims=True))
    router_probs = shifted / jnp.sum(shifted, axis=-1, keepdims=True)
    chosen = routes == jnp.arange(EXPERTS, dtype=jnp.int32)[None, :]
    gate = jnp.sum(jnp.where(chosen, router_probs, 0.0), axis=-1, keepdims=True)
    earlier = (positions[:, None] < positions[None, :]) & (routes == routes[:, 0][None, :])
    slot_index = routes[:, 0] * CAP + jnp.sum(earlier.astype(jnp.int32), axis=0)
    dispatch = (
        slot_index[None, :] == jnp.arange(slot_count, dtype=jnp.int32)[:, None]
    ).astype(bf16)

    def expert_cut(pair, e):
        return [w[:, e * hidden : (e + 1) * hidden] for w in pair]

    up_e = [expert_cut(up_w, e) for e in range(EXPERTS)]
    down_e = [expert_cut(down_w, e) for e in range(EXPERTS)]

    def into(x, pair):
        return dot_nn(x[:, :mid], pair[0]) + dot_nn(x[:, mid:], pair[1])

    def out_of(x, pair):
        return jnp.concatenate([dot_nt(x, w) for w in pair], axis=1)

    def to_tokens(parts):
        return dot_tn(dispatch, jnp.concatenate(parts, axis=0)).astype(bf16)

    dispatched = dot_nn(dispatch, norm_two).astype(bf16)
    scaled_grad = (gate * cot).astype(bf16)
    grad_slots = dot_nn(dispatch, scaled_grad).astype(bf16)
    disp_e = [dispatched[e * CAP : (e + 1) * CAP] for e in range(EXPERTS)]
    slots_e = [grad_slots[e * CAP : (e + 1) * CAP] for e in range(EXPERTS)]

    hidden_act, grad_pre = [], []
    for e in range(EXPERTS):
        value, back = jax.vjp(jax.nn.gelu, into(disp_e[e], up_e[e]))
        hidden_act.append(value.astype(bf16))
        grad_pre.append(back(into(slots_e[e], down_e[e]))[0].astype(bf16))
    grad_rows = to_tokens([out_of(grad_pre[e], up_e[e]).astype(bf16) for e in range(EXPERTS)])
    token_part = to_tokens([out_of(hidden_act[e], down_e[e]).astype(bf16) for e in range(EXPERTS)])
    routed = token_part.astype(f32) + swap(token_part).astype(f32)
    grad_rows = grad_rows.astype(f32) + swap(grad_rows).astype(f32)

    def both_halves(lefts, rights):
        left, right = jnp.stack(lefts), jnp.stack(rights)
        return [
            jnp.einsum(
                "ecd,ecf->edf", left[:, :, cut], right, preferred_element_type=f32
            ).astype(bf16)
            for cut in (slice(0, mid), slice(mid, width))
        ]

    quarter = mid // 2

    def join_core(halves):
        keep, got = halves[0], core_swap(halves[1])
        near = add(keep[..., :quarter, :], got[..., :quarter, :])
        return near, add(keep[..., quarter:, :], got[..., quarter:, :]).astype(bf16)

    def along_z(near, got):
        near = add(near, got)
        part = quarter // 4
        chunk = near[..., part : 2 * part, :].astype(bf16)
        for step in range(3):
            at = (step + 2) % 4
            summed = add(near[..., at * part : (at + 1) * part, :], ring_step(chunk))
            chunk = summed.astype(bf16)
        return summed

    def sum_all(halves):
        return lax.psum_scatter(
            jnp.concatenate(halves, axis=-2), "dp", scatter_dimension=halves[0].ndim - 2, tiled=True
        ).astype(f32)

    down_halves = both_halves(slots_e, hidden_act)
    up_halves = both_halves(disp_e, grad_pre)
    if small_slice:
        down_near, down_far = join_core(down_halves)
        down_got = [across(down_far[e : e + 1]) for e in range(EXPERTS)]
        by_z = (EXPERTS, 2, 4, depth, hidden)
        up_keep, up_came = up_halves[0].reshape(by_z), core_swap(up_halves[1]).reshape(by_z)
        up_chunk = add(up_keep[:, :, 1], up_came[:, :, 1]).astype(bf16)
        first_chunk = up_chunk
        up_first = ring_step(first_chunk)
        for at in (2, 3, 0):
            up_got = up_first if at == 2 else ring_step(up_chunk)
            up_sum = add(up_keep[:, :, at], up_came[:, :, at]) + up_got.astype(f32)
            up_chunk = up_sum.astype(bf16)
        grad_up = add(up_sum[:, 0], across(up_chunk[:, 1]))
        grad_down = along_z(down_near, jnp.concatenate(down_got, axis=0))
    else:
        grad_down, grad_up = sum_all(down_halves), sum_all(up_halves)
    grad_down, grad_up = jnp.swapaxes(grad_down, 0, 1), jnp.swapaxes(grad_up, 0, 1)

    out_rows = own_rows(middle + gate * routed, rank).astype(bf16)
    out_hidden = dot_nt(out_rows, to_here).astype(bf16)
    grad_gate = jnp.sum(cot * routed, axis=-1, keepdims=True)
    picked = jnp.where(chosen, grad_gate, 0.0)
    grad_logits = router_probs * (picked - gate * grad_gate)
    router_wide = router_here.astype(f32)
    grad_norm_two = grad_rows + sum(
        grad_logits[:, e : e + 1] * router_wide[e : e + 1] for e in range(EXPERTS)
    )
    grad_router_here = jnp.stack(
        [
            jnp.sum(norm_two.astype(f32) * grad_logits[:, e : e + 1], axis=0)
            for e in range(EXPERTS)
        ]
    )
    grad_middle_norm, grad_gain_ffn = jax.vjp(normalize, middle, gain_two)[1](grad_norm_two)
    grad_middle = cot + grad_middle_norm

    grad_attended = grad_middle.astype(bf16)
    grad_mixed = into(grad_attended, out_w).astype(bf16)
    if small_slice:
        grad_mixed = tie(grad_mixed, down_far, first_chunk)
    grad_projected, diagonals = call_kernel(
        lambda *refs: backward_kernel(heads, rows, wide, *refs),
        (
            jax.ShapeDtypeStruct((rows, 3 * cols), bf16),
            jax.ShapeDtypeStruct((8, wide), f32),
        ),
        8 * 10**9,
        projected,
        grad_mixed,
        offset_vals,
        doc_col,
        doc_row,
    )
    if small_slice:
        grad_projected = tie(grad_projected, down_got[0], up_first)
    grad_rows_one = out_of(grad_projected, [w[:, : 3 * cols] for w in attn_w]).astype(bf16)
    arrived = swap(own_rows(grad_rows_one, 1 - rank))
    grad_norm_one = own_rows(grad_rows_one, rank).astype(f32) + arrived.astype(f32)
    grad_input_norm, grad_gain_attn = jax.vjp(normalize, own_rows(hid, rank), gain_one)[1](
        grad_norm_one
    )
    grad_input = (own_rows(grad_middle, rank) + grad_input_norm).astype(bf16)
    grad_input = dot_nt(grad_input, to_here).astype(bf16)

    attn_halves = [
        jnp.concatenate(
            [dot_tn(norm_one[:, cut], grad_projected), dot_tn(grad_attended[:, cut], mixed)],
            axis=1,
        ).astype(bf16)
        for cut in (slice(0, mid), slice(mid, width))
    ]
    if small_slice:
        attn_near, attn_far = join_core(attn_halves)
        attention_sums = along_z(attn_near, across(attn_far))
    else:
        attention_sums = sum_all(attn_halves)
    grad_wqkv = attention_sums[:, : 3 * cols].reshape(depth, 3, cols)
    grad_wo = attention_sums[:, 3 * cols :]

    small = jnp.concatenate(
        [grad_gain_attn[None], 0.5 * grad_gain_ffn[None], 0.5 * grad_router_here], axis=0
    )
    small = lax.dot_general(
        small, to_here.astype(f32), (((1,), (1,)), ((), ())), precision=highest
    )
    by_bucket = bucket_onehot(turn - (rows - 1))
    grad_table = jnp.dot(by_bucket.T, diagonals[:heads].T, precision=highest)
    table_full = lax.dynamic_update_slice_in_dim(
        jnp.zeros(bias_table.shape, f32), grad_table, rank * heads, 1
    )
    flat = table_full.reshape(1, -1)
    flat = jnp.pad(flat, ((0, 0), (0, width - flat.shape[1])))
    sums = total(jnp.concatenate([small, flat], axis=0))
    grad_bias = sums[4, : table_full.size].reshape(bias_table.shape)
    return (
        out_hidden,
        grad_input,
        sums[0],
        grad_wqkv,
        grad_wo,
        grad_bias,
        sums[1],
        sums[2:4].T,
        grad_up,
        grad_down,
    )


def solution(mesh):
    placed = (
        P(("dp", "tensor"), None),
        P("dp", None),
        P("dp", None),
        P(),
        P("dp", None, "tensor"),
        P("dp", "tensor"),
        P(),
        P(),
        P(),
        P("dp", None, "tensor"),
        P("dp", None, "tensor"),
        P(("dp", "tensor"), None),
    )
    return jax.shard_map(
        shards,
        mesh=mesh,
        in_specs=placed,
        out_specs=(
            P(("dp", "tensor"), None),
            P(("dp", "tensor"), None),
            P(),
            P("dp", None, "tensor"),
            P("dp", "tensor"),
            P(),
            P(),
            P(),
            P("dp", None, "tensor"),
            P("dp", None, "tensor"),
        ),
        check_vma=False,
    )
```

```python
import jax
import jax.numpy as jnp
import numpy as np
from jax import lax
from jax.experimental import pallas as pl
from jax.experimental.pallas import tpu as pltpu
from jax.sharding import PartitionSpec as P

HD = 64
EXPERTS = 2
BUCKETS = 32
CAP = 192

epsilon = 1e-06
bucket_limits = (12, 16, 23, 32, 46, 64, 91)
highest = lax.Precision.HIGHEST
f32 = jnp.float32
bf16 = jnp.bfloat16


def normalize(values, gains):
    return values * lax.rsqrt(jnp.mean(values * values, axis=-1, keepdims=True) + epsilon) * gains


def bucket_onehot(offsets):
    distance = np.abs(offsets)
    beyond = 8 + sum((distance >= limit).astype(np.int32) for limit in bucket_limits)
    buckets = np.where(distance < 8, distance, beyond) + np.where(offsets > 0, 16, 0)
    return jnp.asarray(buckets[:, None] == np.arange(BUCKETS)[None, :], f32)


def dot_nn(a, b):
    return lax.dot_general(a, b, (((1,), (0,)), ((), ())), preferred_element_type=f32)


def dot_nt(a, b):
    return lax.dot_general(a, b, (((1,), (1,)), ((), ())), preferred_element_type=f32)


def dot_tn(a, b):
    return lax.dot_general(a, b, (((0,), (0,)), ((), ())), preferred_element_type=f32)


def head_probs(q, k, v_ref, same, h, rows, wide):
    raw = dot_nt(q, k) * HD ** (-0.5)
    spread = jnp.broadcast_to(v_ref[h : h + 1, :], (rows, wide))
    bias = pltpu.roll(spread, 0, 1, stride=1, stride_axis=0)[:, :rows]
    scores = jnp.where(same, raw + bias, -1e30)
    shifted = jnp.exp(scores - jnp.max(scores, axis=-1, keepdims=True))
    return shifted / jnp.sum(shifted, axis=-1, keepdims=True)


def forward_kernel(heads, rows, wide, qkv_ref, v_ref, dc_ref, dr_ref, out_ref):
    same = dc_ref[...] == dr_ref[...]
    width = heads * HD
    for h in range(heads):
        cut = slice(h * HD, (h + 1) * HD)
        q = qkv_ref[:, h * HD : (h + 1) * HD]
        k = qkv_ref[:, width + h * HD : width + (h + 1) * HD]
        v = qkv_ref[:, 2 * width + h * HD : 2 * width + (h + 1) * HD]
        probs = head_probs(q, k, v_ref, same, h, rows, wide)
        out_ref[:, cut] = dot_nn(probs.astype(bf16), v).astype(bf16)


def backward_kernel(heads, rows, wide, qkv_ref, gm_ref, v_ref, dc_ref, dr_ref, gp_ref, diag_ref):
    same = dc_ref[...] == dr_ref[...]
    width = heads * HD
    flip = (
        lax.broadcasted_iota(jnp.int32, (rows, rows), 0)
        + lax.broadcasted_iota(jnp.int32, (rows, rows), 1)
        == rows - 1
    ).astype(f32).astype(bf16)
    diag_ref[...] = jnp.zeros_like(diag_ref)
    for h in range(heads):
        q = qkv_ref[:, h * HD : (h + 1) * HD]
        k = qkv_ref[:, width + h * HD : width + (h + 1) * HD]
        v = qkv_ref[:, 2 * width + h * HD : 2 * width + (h + 1) * HD]
        g = gm_ref[:, h * HD : (h + 1) * HD]
        probs = head_probs(q, k, v_ref, same, h, rows, wide)
        gv = dot_tn(probs.astype(bf16), g)
        gprobs = dot_nt(g, v)
        ds = probs * (gprobs - jnp.sum(probs * gprobs, axis=-1, keepdims=True))
        low = ds.astype(bf16)
        gq = dot_nn(low, k) * HD ** (-0.5)
        gk = dot_tn(low, q) * HD ** (-0.5)
        gp_ref[:, h * HD : (h + 1) * HD] = gq.astype(bf16)
        gp_ref[:, width + h * HD : width + (h + 1) * HD] = gk.astype(bf16)
        gp_ref[:, 2 * width + h * HD : 2 * width + (h + 1) * HD] = gv.astype(bf16)
        turned = dot_nn(flip, low)
        padded = jnp.concatenate([turned, jnp.zeros((rows, wide - rows), f32)], axis=1)
        rolled = pltpu.roll(padded, 0, 1, stride=1, stride_axis=0)
        diag_ref[h : h + 1, :] = jnp.sum(rolled, axis=0, keepdims=True)


def call_kernel(body, outs, flops, *operands):
    return pl.pallas_call(
        body,
        out_shape=outs,
        in_specs=[pl.BlockSpec(memory_space=pltpu.VMEM)] * len(operands),
        out_specs=jax.tree.map(lambda _: pl.BlockSpec(memory_space=pltpu.VMEM), outs),
        compiler_params=pltpu.CompilerParams(vmem_limit_bytes=40 * 2**20),
        cost_estimate=pl.CostEstimate(flops=flops, bytes_accessed=2**21, transcendentals=2**20),
    )(*operands)


def tie(x, *others):
    return lax.optimization_barrier((x,) + others)[0]


def add(a, b):
    return a.astype(f32) + b.astype(f32)


def make_links(dp):
    def by(mask):
        return [(i, i ^ mask) for i in range(dp)]

    ring = [(i, (i + 4) % dp) for i in range(dp)]

    def move(x, perm):
        return lax.ppermute(x, "dp", perm)

    def ring_step(x):
        return move(x, ring)

    def across(x):
        return move(x, by(2))

    def core(x):
        return move(x, by(1))

    return ring_step, across, core, total_of(dp, move, by)


def total_of(dp, move, by):
    def total(x):
        if dp != 16:
            return lax.psum(x, ("dp", "tensor"))
        x = x + lax.ppermute(x, "tensor", [(0, 1), (1, 0)])
        for mask in (1, 2, 4, 8):
            x = x + move(x, by(mask))
        return x

    return total


def shards(
    hidden_in,
    lengths,
    routes,
    gain_attn,
    wqkv,
    wo_t,
    bias_table,
    gain_ffn,
    router,
    w_up,
    w_down_t,
    cotangent,
):
    dp = lax.axis_size("dp")
    ring_step, across, core_swap, total = make_links(dp)
    small_slice = dp == 16
    rank = lax.axis_index("tensor")
    half_rows = hidden_in.shape[0]
    rows = routes.shape[0]
    width = hidden_in.shape[1]
    mid = width // 2
    cols = wqkv.shape[2]
    heads = cols // HD
    hidden = w_up.shape[2]
    depth = wqkv.shape[0]
    slot_count = EXPERTS * CAP
    wide = 128 * (-(-2 * rows // 128))

    def swap(x):
        return lax.ppermute(x, "tensor", [(0, 1), (1, 0)])

    def whole_rows(own):
        other = swap(own)
        return jnp.where(
            rank == 0, jnp.concatenate([own, other]), jnp.concatenate([other, own])
        )

    def own_rows(x, who):
        return lax.dynamic_slice_in_dim(x, who * half_rows, half_rows, 0)

    attn_own = jnp.concatenate([wqkv.reshape(depth, 3 * cols), wo_t], axis=1)
    experts_own = jnp.concatenate(
        [w_up.reshape(depth, EXPERTS * hidden), w_down_t.reshape(depth, EXPERTS * hidden)], axis=1
    )
    parts = EXPERTS * hidden
    if small_slice:
        held, sides = [attn_own], [across(attn_own)]
        for step in range(3):
            held.append(ring_step(held[-1]))
            sides.append(across(held[-1]))
        near = jnp.concatenate(held + sides, axis=0)
        attn_w = (near, core_swap(near))
        begun = tie(experts_own, held[1])
        big_held, big_sides = [begun, ring_step(begun)], [across(begun)]
        big_held[1], big_sides[0], _ = lax.optimization_barrier(
            (big_held[1], big_sides[0], attn_w[1])
        )
        for step in range(2):
            big_held.append(ring_step(big_held[-1]))
            big_sides.append(across(big_held[-2]))
    else:
        attn_all = lax.all_gather(attn_own, "dp", axis=0, tiled=True)
        experts_all = lax.all_gather(experts_own, "dp", axis=0, tiled=True)
        attn_w = (attn_all[:mid], attn_all[mid:])
        up_w = (experts_all[:mid, :parts], experts_all[mid:, :parts])
        down_w = (experts_all[:mid, parts:], experts_all[mid:, parts:])

    place = jnp.arange(width, dtype=jnp.int32)
    if small_slice:
        me = lax.axis_index("dp")
        z, y, core = me // 4, (me // 2) % 2, me % 2
        from_core = (core + place // mid) % 2
        from_y = (y + (place // (mid // 2)) % 2) % 2
        from_z = (z + 4 - (place // depth) % 4) % 4
        origin = (from_z * 4 + from_y * 2 + from_core) * depth + place % depth
    else:
        origin = place
    to_here = (place[:, None] == origin[None, :]).astype(bf16)

    hid = dot_nn(whole_rows(hidden_in), to_here)
    cot = dot_nn(whole_rows(cotangent), to_here)
    vectors = jnp.concatenate(
        [gain_attn[None], gain_ffn[None], router.astype(f32).T], axis=0
    )
    vectors = jnp.dot(vectors, to_here.astype(f32), precision=highest)
    gain_one, gain_two, router_here = vectors[0], vectors[1], vectors[2:].astype(bf16)

    positions = jnp.arange(rows, dtype=jnp.int32)
    first, second = lengths[0, 0], lengths[0, 0] + lengths[0, 1]
    docs = (
        (positions >= first).astype(jnp.int32)
        + (positions >= second).astype(jnp.int32)
        + (positions >= second + lengths[0, 2]).astype(jnp.int32)
    )
    doc_col, doc_row = docs[:, None], docs[None, :]
    table_cols = lax.dynamic_slice_in_dim(bias_table, rank * heads, heads, 1)
    turn = np.arange(wide)
    spread = bucket_onehot(np.where(turn < rows, turn, turn - wide))
    offset_vals = jnp.dot(table_cols.T, spread.T, precision=highest)

    norm_one = normalize(hid, gain_one).astype(bf16)
    projected = dot_nn(norm_one[:, :mid], attn_w[0][:, : 3 * cols])
    projected = projected + dot_nn(norm_one[:, mid:], attn_w[1][:, : 3 * cols])
    projected = projected.astype(bf16)
    mixed = call_kernel(
        lambda *refs: forward_kernel(heads, rows, wide, *refs),
        jax.ShapeDtypeStruct((rows, cols), bf16),
        5 * 10**9,
        projected,
        offset_vals,
        doc_col,
        doc_row,
    )
    out_w = [w[:, 3 * cols :] for w in attn_w]
    attended_part = jnp.concatenate([dot_nt(mixed, w) for w in out_w], axis=1).astype(bf16)
    attended_got = swap(attended_part)
    middle = hid + add(attended_part, attended_got)
    if small_slice:
        big_sides.append(across(tie(big_held[-1], attended_got)))
        pieces = big_held + big_sides
        near_up = jnp.concatenate([p[:, :parts] for p in pieces], axis=0)
        near_down = jnp.concatenate([p[:, parts:] for p in pieces], axis=0)
        up_w = (near_up, core_swap(near_up))
        down_w = (near_down, core_swap(near_down))

    norm_two = normalize(middle, gain_two).astype(bf16)
    logits = dot_nt(norm_two, router_here)
    shifted = jnp.exp(logits - jnp.max(logits, axis=-1, keepdims=True))
    router_probs = shifted / jnp.sum(shifted, axis=-1, keepdims=True)
    chosen = routes == jnp.arange(EXPERTS, dtype=jnp.int32)[None, :]
    gate = jnp.sum(jnp.where(chosen, router_probs, 0.0), axis=-1, keepdims=True)
    earlier = (positions[:, None] < positions[None, :]) & (routes == routes[:, 0][None, :])
    slot_index = routes[:, 0] * CAP + jnp.sum(earlier.astype(jnp.int32), axis=0)
    dispatch = (
        slot_index[None, :] == jnp.arange(slot_count, dtype=jnp.int32)[:, None]
    ).astype(bf16)

    def expert_cut(pair, e):
        return [w[:, e * hidden : (e + 1) * hidden] for w in pair]

    up_e = [expert_cut(up_w, e) for e in range(EXPERTS)]
    down_e = [expert_cut(down_w, e) for e in range(EXPERTS)]

    def into(x, pair):
        return dot_nn(x[:, :mid], pair[0]) + dot_nn(x[:, mid:], pair[1])

    def out_of(x, pair):
        return jnp.concatenate([dot_nt(x, w) for w in pair], axis=1)

    def to_tokens(parts):
        return dot_tn(dispatch, jnp.concatenate(parts, axis=0)).astype(bf16)

    dispatched = dot_nn(dispatch, norm_two).astype(bf16)
    scaled_grad = (gate * cot).astype(bf16)
    grad_slots = dot_nn(dispatch, scaled_grad).astype(bf16)
    disp_e = [dispatched[e * CAP : (e + 1) * CAP] for e in range(EXPERTS)]
    slots_e = [grad_slots[e * CAP : (e + 1) * CAP] for e in range(EXPERTS)]

    hidden_act, grad_pre = [], []
    for e in range(EXPERTS):
        value, back = jax.vjp(jax.nn.gelu, into(disp_e[e], up_e[e]))
        hidden_act.append(value.astype(bf16))
        grad_pre.append(back(into(slots_e[e], down_e[e]))[0].astype(bf16))
    grad_rows = to_tokens([out_of(grad_pre[e], up_e[e]).astype(bf16) for e in range(EXPERTS)])
    token_part = to_tokens([out_of(hidden_act[e], down_e[e]).astype(bf16) for e in range(EXPERTS)])
    routed = token_part.astype(f32) + swap(token_part).astype(f32)
    grad_rows = grad_rows.astype(f32) + swap(grad_rows).astype(f32)

    def both_halves(lefts, rights):
        left, right = jnp.stack(lefts), jnp.stack(rights)
        return [
            jnp.einsum(
                "ecd,ecf->edf", left[:, :, cut], right, preferred_element_type=f32
            ).astype(bf16)
            for cut in (slice(0, mid), slice(mid, width))
        ]

    quarter = mid // 2

    def join_core(halves):
        keep, got = halves[0], core_swap(halves[1])
        near = add(keep[..., :quarter, :], got[..., :quarter, :])
        return near, add(keep[..., quarter:, :], got[..., quarter:, :]).astype(bf16)

    def along_z(near, got):
        near = add(near, got)
        part = quarter // 4
        chunk = near[..., part : 2 * part, :].astype(bf16)
        steps = []
        for step in range(3):
            at = (step + 2) % 4
            steps.append(ring_step(chunk))
            summed = add(near[..., at * part : (at + 1) * part, :], steps[-1])
            chunk = summed.astype(bf16)
        return summed, steps[0]

    def sum_all(halves):
        return lax.psum_scatter(
            jnp.concatenate(halves, axis=-2), "dp", scatter_dimension=halves[0].ndim - 2, tiled=True
        ).astype(f32)

    down_halves = both_halves(slots_e, hidden_act)
    up_halves = both_halves(disp_e, grad_pre)
    if small_slice:
        down_near, down_far = join_core(down_halves)
        down_got = [across(down_far[e : e + 1]) for e in range(EXPERTS)]
        by_z = (EXPERTS, 2, 4, depth, hidden)
        up_keep, up_came = up_halves[0].reshape(by_z), core_swap(up_halves[1]).reshape(by_z)
        up_chunk = add(up_keep[:, :, 1], up_came[:, :, 1]).astype(bf16)
        first_chunk = up_chunk
        up_first = ring_step(first_chunk)
        for at in (2, 3, 0):
            up_got = up_first if at == 2 else ring_step(up_chunk)
            up_sum = add(up_keep[:, :, at], up_came[:, :, at]) + up_got.astype(f32)
            up_chunk = up_sum.astype(bf16)
        grad_up = add(up_sum[:, 0], across(up_chunk[:, 1]))
        grad_down, _ = along_z(down_near, jnp.concatenate(down_got, axis=0))
    else:
        grad_down, grad_up = sum_all(down_halves), sum_all(up_halves)
    grad_down, grad_up = jnp.swapaxes(grad_down, 0, 1), jnp.swapaxes(grad_up, 0, 1)

    out_rows = own_rows(middle + gate * routed, rank).astype(bf16)
    out_hidden = dot_nt(out_rows, to_here).astype(bf16)
    grad_gate = jnp.sum(cot * routed, axis=-1, keepdims=True)
    picked = jnp.where(chosen, grad_gate, 0.0)
    grad_logits = router_probs * (picked - gate * grad_gate)
    router_wide = router_here.astype(f32)
    grad_norm_two = grad_rows + sum(
        grad_logits[:, e : e + 1] * router_wide[e : e + 1] for e in range(EXPERTS)
    )
    grad_router_here = jnp.stack(
        [
            jnp.sum(norm_two.astype(f32) * grad_logits[:, e : e + 1], axis=0)
            for e in range(EXPERTS)
        ]
    )
    grad_middle_norm, grad_gain_ffn = jax.vjp(normalize, middle, gain_two)[1](grad_norm_two)
    grad_middle = cot + grad_middle_norm

    grad_attended = grad_middle.astype(bf16)
    grad_mixed = into(grad_attended, out_w).astype(bf16)
    if small_slice:
        grad_mixed = tie(grad_mixed, down_far, first_chunk)
    grad_projected, diagonals = call_kernel(
        lambda *refs: backward_kernel(heads, rows, wide, *refs),
        (
            jax.ShapeDtypeStruct((rows, 3 * cols), bf16),
            jax.ShapeDtypeStruct((8, wide), f32),
        ),
        8 * 10**9,
        projected,
        grad_mixed,
        offset_vals,
        doc_col,
        doc_row,
    )
    if small_slice:
        grad_projected = tie(grad_projected, down_got[0], up_first)
    grad_rows_one = out_of(grad_projected, [w[:, : 3 * cols] for w in attn_w]).astype(bf16)
    arrived = swap(own_rows(grad_rows_one, 1 - rank))
    grad_norm_one = own_rows(grad_rows_one, rank).astype(f32) + arrived.astype(f32)
    grad_input_norm, grad_gain_attn = jax.vjp(normalize, own_rows(hid, rank), gain_one)[1](
        grad_norm_one
    )
    grad_input = (own_rows(grad_middle, rank) + grad_input_norm).astype(bf16)
    grad_input = dot_nt(grad_input, to_here).astype(bf16)

    attn_halves = [
        jnp.concatenate(
            [dot_tn(norm_one[:, cut], grad_projected), dot_tn(grad_attended[:, cut], mixed)],
            axis=1,
        ).astype(bf16)
        for cut in (slice(0, mid), slice(mid, width))
    ]
    if small_slice:
        attn_near, attn_far = join_core(attn_halves)
        attention_sums, attn_first = along_z(attn_near, across(attn_far))
    else:
        attention_sums = sum_all(attn_halves)
    grad_wqkv = attention_sums[:, : 3 * cols].reshape(depth, 3, cols)
    grad_wo = attention_sums[:, 3 * cols :]

    small = jnp.concatenate(
        [grad_gain_attn[None], 0.5 * grad_gain_ffn[None], 0.5 * grad_router_here], axis=0
    )
    if small_slice:
        small = tie(small, attn_first)
    small = lax.dot_general(
        small, to_here.astype(f32), (((1,), (1,)), ((), ())), precision=highest
    )
    by_bucket = bucket_onehot(turn - (rows - 1))
    grad_table = jnp.dot(by_bucket.T, diagonals[:heads].T, precision=highest)
    table_full = lax.dynamic_update_slice_in_dim(
        jnp.zeros(bias_table.shape, f32), grad_table, rank * heads, 1
    )
    flat = table_full.reshape(1, -1)
    flat = jnp.pad(flat, ((0, 0), (0, width - flat.shape[1])))
    sums = total(jnp.concatenate([small, flat], axis=0))
    grad_bias = sums[4, : table_full.size].reshape(bias_table.shape)
    return (
        out_hidden,
        grad_input,
        sums[0],
        grad_wqkv,
        grad_wo,
        grad_bias,
        sums[1],
        sums[2:4].T,
        grad_up,
        grad_down,
    )


def solution(mesh):
    placed = (
        P(("dp", "tensor"), None),
        P("dp", None),
        P("dp", None),
        P(),
        P("dp", None, "tensor"),
        P("dp", "tensor"),
        P(),
        P(),
        P(),
        P("dp", None, "tensor"),
        P("dp", None, "tensor"),
        P(("dp", "tensor"), None),
    )
    return jax.shard_map(
        shards,
        mesh=mesh,
        in_specs=placed,
        out_specs=(
            P(("dp", "tensor"), None),
            P(("dp", "tensor"), None),
            P(),
            P("dp", None, "tensor"),
            P("dp", "tensor"),
            P(),
            P(),
            P(),
            P("dp", None, "tensor"),
            P("dp", None, "tensor"),
        ),
        check_vma=False,
    )
```
